32 devices in a mesh: groups: 2 (over x), row: 16 (over z, y, core).
Axes of the slice: x: 2, y: 2, z: 4, core: 2. Of those that a mesh axis runs over, the one named last changes fastest.
Arguments:
- level0_tokens: bfloat16 [256, 128, 256], P(('groups', 'row')), parts along dimension 0, may hold values from -6 to 6
- level0_mod: float32 [6, 256], P('groups'), parts along dimension 0, may hold values from -3 to 3
- level0_qkv: bfloat16 [256, 768], replicated, may hold values from -2 to 2
- level0_out: bfloat16 [256, 256], replicated, may hold values from -0.375 to 0.375
- level0_merge: bfloat16 [1024, 512], replicated, may hold values from -0.1875 to 0.1875
- level1_mod: float32 [6, 512], P('groups'), parts along dimension 0, may hold values from -3 to 3
- level1_qkv: bfloat16 [512, 1536], replicated, may hold values from -2 to 2
- level1_out: bfloat16 [512, 512], replicated, may hold values from -0.25 to 0.25
- level1_merge: bfloat16 [2048, 1024], replicated, may hold values from -0.125 to 0.125
- level2_mod: float32 [6, 1024], P('groups'), parts along dimension 0, may hold values from -3 to 3
- level2_qkv: bfloat16 [1024, 1536], replicated, may hold values from -2 to 2
- level2_out: bfloat16 [512, 1024], replicated, may hold values from -0.25 to 0.25
Outputs:
- level2_result: bfloat16 [64, 32, 1024], P(('groups', 'row')), parts along dimension 0
The draws below stay inside these ranges and needn't reach their ends.
There are 2 independent parts, one for each index of `groups`. The reference program is written for one: setup_inputs(seed, part) draws one part's arguments, and reference() takes and returns one part's arrays. A program takes and returns all parts, laid end to end along the dimension named above; an argument that names none is the same for every part. Nothing has to cross between parts.
All inputs are finite; a program needn't handle non-finite values.
Results may differ from the reference program's by a relative error of at most 0.015.
Values may be sent and summed in bfloat16 or wider, within the bound.
A program may use at most 192 MiB of HBM per device.

```python
import math
import jax
import jax.numpy as jnp
from jax import lax

C0 = 256
C1 = 512
C2 = 1024
DH = 64
HEADS2 = 8
W0 = 128
H0 = 128


def drawn_table(key, row_count, col_total):
    table = jax.random.normal(key, (row_count, col_total), jnp.float32) / math.sqrt(row_count)
    return jnp.clip(table, -2.0, 2.0).astype(jnp.bfloat16)


def draw_level0_qkv(key, part):
    key = jax.random.fold_in(key, 11)
    return drawn_table(key, C0, 3 * C0)


def draw_level1_qkv(key, part):
    key = jax.random.fold_in(key, 23)
    return drawn_table(key, C1, 3 * C1)


def draw_level2_qkv(key, part):
    key = jax.random.fold_in(key, 37)
    return drawn_table(key, C2, 3 * HEADS2 * DH)


def levels(rng, extent, cuts, low, largest):
    factor_of = 1.0
    for dim, shards_of in cuts:
        heights = jax.random.uniform(jax.random.fold_in(jax.random.fold_in(rng, 6), dim), (shards_of,), jnp.float32, low / len(cuts), largest / len(cuts))
        factor_of = factor_of * jnp.repeat(jnp.exp(heights), extent[dim] // shards_of).reshape((-1,) + (1,) * (len(extent) - 1 - dim))
    return factor_of


def gaussian(key, shape, scale, limit, pieces=(), kind=jnp.bfloat16):
    entries = scale * jax.random.normal(key, shape, jnp.float32)
    if pieces:
        entries = entries * levels(key, shape, pieces, -0.22, 0.18)
    return jnp.clip(entries, -limit, limit).astype(kind)


def setup_inputs(seed: int = 0, part: int = 0) -> dict:
    arg_keys = jax.random.split(jax.random.key(seed), 13)
    part_splits = jax.random.split(jax.random.fold_in(arg_keys[12], part), 13)
    level0_tokens = gaussian(part_splits[0], (H0, W0, C0), 1.0, 6.0, ((0, 16),))
    level0_mod = gaussian(part_splits[1], (3, C0), 0.5, 3.0, (), jnp.float32)
    level0_qkv = draw_level0_qkv(jax.random.fold_in(arg_keys[12], 71), part)
    level0_out = gaussian(arg_keys[3], (C0, C0), C0 ** -0.5, 0.375)
    level0_merge = gaussian(arg_keys[4], (4 * C0, C1), (4 * C0) ** -0.5, 0.1875)
    level1_mod = gaussian(part_splits[5], (3, C1), 0.5, 3.0, (), jnp.float32)
    level1_qkv = draw_level1_qkv(jax.random.fold_in(arg_keys[12], 71), part)
    level1_out = gaussian(arg_keys[7], (C1, C1), C1 ** -0.5, 0.25)
    level1_merge = gaussian(arg_keys[8], (4 * C1, C2), (4 * C1) ** -0.5, 0.125)
    level2_mod = gaussian(part_splits[9], (3, C2), 0.5, 3.0, (), jnp.float32)
    level2_qkv = draw_level2_qkv(jax.random.fold_in(arg_keys[12], 71), part)
    level2_out = gaussian(arg_keys[11], (HEADS2 * DH, C2), (HEADS2 * DH) ** -0.5, 0.25)
    return {"level0_tokens": level0_tokens, "level0_mod": level0_mod, "level0_qkv": level0_qkv, "level0_out": level0_out, "level0_merge": level0_merge, "level1_mod": level1_mod, "level1_qkv": level1_qkv, "level1_out": level1_out, "level1_merge": level1_merge, "level2_mod": level2_mod, "level2_qkv": level2_qkv, "level2_out": level2_out}


EPSILON = 1e-06
NEGATIVE = -1e+30

def modulate(tokens, modulation):
    values = tokens.astype(jnp.float32)
    center = values - lax.optimization_barrier(jnp.mean(values, axis=-1, keepdims=True))
    spread = lax.optimization_barrier(jnp.mean(center * center, axis=-1, keepdims=True))
    normed = center * lax.rsqrt(spread + EPSILON)
    return (normed * (1.0 + modulation[1]) + modulation[0]).astype(jnp.bfloat16)

def project(tokens, weight):
    return jnp.dot(tokens, weight, preferred_element_type=jnp.float32).astype(jnp.bfloat16)

def residual_gate(tokens, modulation, attended, w_out):
    branch = jnp.dot(attended, w_out, preferred_element_type=jnp.float32)
    return (tokens.astype(jnp.float32) + modulation[2] * branch).astype(jnp.bfloat16)

def merge_tokens(tokens, w_merge):
    row_count, col_count, feat_width = tokens.shape
    folded = tokens.reshape(row_count // 2, 2, col_count // 2, 2, feat_width).transpose(0, 2, 1, 3, 4)
    folded = folded.reshape(row_count // 2, col_count // 2, 4 * feat_width)
    return project(folded, w_merge)

def window_attention(queries, key_vals, head_count):
    row_count, col_count, feat_width = queries.shape
    head_size = feat_width // head_count
    q_heads = queries.astype(jnp.float32).reshape(row_count, col_count, head_count, head_size)
    padded = jnp.pad(key_vals.astype(jnp.float32).reshape(row_count, col_count, 2, head_count, head_size), ((3, 3), (3, 3), (0, 0), (0, 0), (0, 0)))
    valid = jnp.pad(jnp.ones((row_count, col_count), jnp.float32), 3)
    score_list = []
    for down in range(7):
        for across in range(7):
            shifted = padded[down:down + row_count, across:across + col_count, 0]
            scores = lax.optimization_barrier(jnp.sum(q_heads * shifted, axis=-1)) * head_size ** (-0.5)
            inside = valid[down:down + row_count, across:across + col_count]
            score_list.append(jnp.where(inside[..., None] > 0, scores, NEGATIVE))
    stacked = jnp.stack(score_list, 0)
    row_max = lax.optimization_barrier(jnp.max(stacked, axis=0))
    exponent = jnp.exp(stacked - row_max[None])
    denominator = lax.optimization_barrier(jnp.sum(exponent, axis=0))
    rounded = lax.optimization_barrier(exponent.astype(jnp.bfloat16)).astype(jnp.float32)
    summed = jnp.zeros((row_count, col_count, head_count, head_size), jnp.float32)
    position = 0
    for down in range(7):
        for across in range(7):
            summed = summed + rounded[position][..., None] * padded[down:down + row_count, across:across + col_count, 1]
            position = position + 1
    attended = summed / denominator[..., None]
    return attended.reshape(row_count, col_count, feat_width).astype(jnp.bfloat16)

def local_level(tokens, modulation, w_qkv, w_out):
    feat_width = tokens.shape[2]
    hidden = project(modulate(tokens, modulation), w_qkv)
    attended = window_attention(hidden[..., :feat_width], hidden[..., feat_width:], feat_width // DH)
    return residual_gate(tokens, modulation, attended, w_out)

def global_level(tokens, modulation, w_qkv, w_out):
    row_count, col_count, feat_width = tokens.shape
    inner = w_qkv.shape[1] // 3
    count = row_count * col_count
    hidden = project(modulate(tokens, modulation), w_qkv).reshape(count, 3, HEADS2, DH)
    by_head = hidden.transpose(2, 1, 0, 3)

    def one_head(parts):
        scores = jnp.dot(parts[0], parts[1].T, preferred_element_type=jnp.float32) * DH ** (-0.5)
        row_max = lax.optimization_barrier(jnp.max(scores, axis=1, keepdims=True))
        exponent = jnp.exp(scores - row_max)
        denominator = lax.optimization_barrier(jnp.sum(exponent, axis=1, keepdims=True))
        summed = jnp.dot(exponent.astype(jnp.bfloat16), parts[2], preferred_element_type=jnp.float32)
        return (summed / denominator).astype(jnp.bfloat16)
    results = lax.map(one_head, by_head)
    attended = results.transpose(1, 0, 2).reshape(row_count, col_count, inner)
    return residual_gate(tokens, modulation, attended, w_out)

def reference(level0_tokens, level0_mod, level0_qkv, level0_out, level0_merge, level1_mod, level1_qkv, level1_out, level1_merge, level2_mod, level2_qkv, level2_out):
    fine_out = local_level(level0_tokens, level0_mod, level0_qkv, level0_out)
    middle = merge_tokens(fine_out, level0_merge)
    middle_out = local_level(middle, level1_mod, level1_qkv, level1_out)
    coarse = merge_tokens(middle_out, level1_merge)
    return global_level(coarse, level2_mod, level2_qkv, level2_out)
```

```python
import functools

import jax
import jax.numpy as jnp
from jax import lax
from jax.experimental import pallas as pl
from jax.experimental.pallas import tpu as pltpu
from jax.sharding import PartitionSpec as P

DH = 64
HEADS2 = 8
HALO = 3
PAD = 8
TILE = 32
SPAN = TILE + 2 * PAD
LANES = 256
EPSILON = 1e-06
NEGATIVE = -1e30
MESH = pl.DeviceIdType.MESH
F32 = jnp.float32
BF16 = jnp.bfloat16


def modulate(values, mod_ref):
    center = values - jnp.mean(values, axis=-1, keepdims=True)
    spread = jnp.mean(center * center, axis=-1, keepdims=True)
    normed = center * lax.rsqrt(spread + EPSILON)
    return (normed * (1.0 + mod_ref[1:2, :]) + mod_ref[0:1, :]).astype(BF16)


def dot(a, b):
    return jnp.dot(a, b, preferred_element_type=F32)


def dot_t(a, b):
    return lax.dot_general(a, b, (((1,), (1,)), ((), ())), preferred_element_type=F32)


def key_position(count):
    n = lax.broadcasted_iota(jnp.int32, (1, count), 1)
    row = jnp.zeros((1, count), jnp.int32)
    for step in range(1, count // SPAN):
        row = row + (n >= step * SPAN).astype(jnp.int32)
    return row, n - row * SPAN


def window_bias(rows):
    k_row, k_col = key_position((rows + 2 * HALO) * SPAN)
    m = lax.broadcasted_iota(jnp.int32, (rows * TILE, 1), 0)
    row_gap = k_row - m // TILE
    col_gap = k_col - PAD - m % TILE
    near = (row_gap >= 0) & (row_gap <= 2 * HALO) & (col_gap >= -HALO) & (col_gap <= HALO)
    return jnp.where(near, 0.0, NEGATIVE).astype(F32)


def project_rows(x, mod_ref, w_ref, row_count, col_count, first):
    h = modulate(x.reshape(row_count * col_count, x.shape[-1]).astype(F32), mod_ref)
    return dot(h, w_ref[:, first:])


def store_kv(kv, k_ref, v_ref, at, row_count, col_count):
    feat = kv.shape[1] // 2
    zero = jnp.zeros((row_count, PAD, 2 * feat), F32)
    kv = kv.reshape(row_count, col_count, 2 * feat)
    kv = jnp.concatenate([zero, kv, zero], axis=1).astype(BF16)
    k_ref[at : at + row_count] = kv[:, :, :feat]
    v_ref[at : at + row_count] = kv[:, :, feat:]


def attend(q_ref, k_ref, v_ref, o_ref, bias, r0, c0, l0, rows, row_start, total_rows, col_count):
    keys = (rows + 2 * HALO) * SPAN
    m = rows * TILE
    heads = LANES // DH
    lane_head = lax.broadcasted_iota(jnp.int32, (1, LANES), 1) // DH
    k_row, k_col = key_position(keys)
    g_row = row_start + r0 + k_row - HALO
    g_col = c0 + k_col - PAD
    inside = (g_row >= 0) & (g_row < total_rows) & (g_col >= 0) & (g_col < col_count)
    bias = bias + jnp.where(inside, 0.0, NEGATIVE).astype(F32)
    q = q_ref[r0 : r0 + rows, pl.ds(c0, TILE), l0 : l0 + LANES].reshape(m, LANES)
    k = k_ref[r0 : r0 + rows + 2 * HALO, pl.ds(c0, SPAN), l0 : l0 + LANES].reshape(keys, LANES)
    v = v_ref[r0 : r0 + rows + 2 * HALO, pl.ds(c0, SPAN), l0 : l0 + LANES].reshape(keys, LANES)
    out = jnp.zeros((m, LANES), F32)
    stacked = jnp.concatenate(
        [q * (lane_head == h).astype(F32).astype(BF16) for h in range(heads)], axis=0
    )
    s = dot_t(stacked, k).reshape(heads, m, keys) + bias[None]
    top = jnp.max(s, axis=-1, keepdims=True)
    e = jnp.exp(s - top)
    total = jnp.sum(e, axis=-1, keepdims=True)
    o = dot(e.astype(BF16).reshape(heads * m, keys), v).reshape(heads, m, LANES) / total
    for h in range(heads):
        out = jnp.where(lane_head == h, o[h], out)
    o_ref[r0 : r0 + rows, pl.ds(c0, TILE), l0 : l0 + LANES] = out.astype(BF16).reshape(
        rows, TILE, LANES
    )


def gated(x, mod_ref, attended, w_ref):
    return (x.astype(F32) + mod_ref[2:3, :] * dot(attended, w_ref[...])).astype(BF16)


def merge(y, w_ref, row_count, col_count):
    half = col_count // 2
    i = lax.broadcasted_iota(jnp.int32, (col_count, col_count), 0)
    j = lax.broadcasted_iota(jnp.int32, (col_count, col_count), 1)
    source = jnp.where(i < half, 2 * i, 2 * (i - half) + 1)
    pick = (source == j).astype(F32).astype(BF16)
    lines = []
    for r in range(0, row_count, 2):
        parts = []
        for u in (r, r + 1):
            both = dot(pick, y[u * col_count : (u + 1) * col_count]).astype(BF16)
            parts += [both[:half], both[half:]]
        lines.append(jnp.concatenate(parts, axis=1))
    return dot(jnp.concatenate(lines, axis=0), w_ref[...]).astype(BF16)


def remote(src, dst, send, recv, peer):
    return pltpu.make_async_remote_copy(
        src_ref=src, dst_ref=dst, send_sem=send, recv_sem=recv,
        device_id={"row": peer}, device_id_type=MESH,
    )


def halo_copies(n, me, src, dst, send, recv, own_rows, act):
    down = remote(
        src.at[pl.ds(own_rows - HALO, HALO)], dst.at[pl.ds(0, HALO)],
        send.at[0], recv.at[0], jnp.minimum(me + 1, n - 1),
    )
    up = remote(
        src.at[pl.ds(0, HALO)], dst.at[pl.ds(HALO, HALO)],
        send.at[1], recv.at[1], jnp.maximum(me - 1, 0),
    )

    @pl.when(me < n - 1)
    def _():
        if act == "start":
            down.start()
        elif act == "send":
            down.wait_send()
        else:
            up.wait_recv()

    @pl.when(me > 0)
    def _():
        if act == "start":
            up.start()
        elif act == "send":
            up.wait_send()
        else:
            down.wait_recv()


def kernel(
    n,
    tok, mod0, w_qkv0, w_out0, w_merge0, mod1, w_qkv1, w_out1, w_merge1, mod2, w_qkv2, w_out2,
    result,
    qkv0, out0, merge0, qkv1, out1, merge1, qkv2, out2, w_sem,
    x0, x0_halo, q0, k0, v0, a0, x1, x1_halo, q1, k1, v1, a1,
    kv_out, q_out, o_out, kv_all, q_all, o_all,
    h0_send, h0_recv, h1_send, h1_recv, kv_send, kv_recv, q_send, q_recv, o_send, o_recv,
):
    rows0, cols0, feat0 = tok.shape
    rows1, cols1, feat1 = rows0 // 2, cols0 // 2, x1.shape[2]
    rows2, cols2 = rows1 // 2, cols1 // 2
    count2 = rows2 * cols2
    me = lax.axis_index("row")
    scale = DH**-0.5

    own = pltpu.make_async_copy(tok, x0, w_sem.at[8])
    own.start()
    loads = [
        pltpu.make_async_copy(src, dst, w_sem.at[i])
        for i, (src, dst) in enumerate(
            [(w_qkv0, qkv0), (w_out0, out0), (w_merge0, merge0), (w_qkv1, qkv1),
             (w_out1, out1), (w_merge1, merge1), (w_qkv2, qkv2), (w_out2, out2)]
        )
    ]
    for load in loads:
        load.start()

    barrier = pltpu.get_barrier_semaphore()

    def greet(p, carry):
        pl.semaphore_signal(
            barrier, inc=1, device_id={"row": lax.rem(me + p, n)}, device_id_type=MESH
        )
        return carry

    lax.fori_loop(1, n, greet, 0)

    @pl.when(me == 0)
    def _():
        x0_halo[0:HALO] = jnp.zeros((HALO, cols0, feat0), BF16)
        x1_halo[0:HALO] = jnp.zeros((HALO, cols1, feat1), BF16)

    @pl.when(me == n - 1)
    def _():
        x0_halo[HALO:] = jnp.zeros((HALO, cols0, feat0), BF16)
        x1_halo[HALO:] = jnp.zeros((HALO, cols1, feat1), BF16)

    own.wait()
    pl.semaphore_wait(barrier, n - 1)
    halo_copies(n, me, x0, x0_halo, h0_send, h0_recv, rows0, "start")

    loads[0].wait()
    chunk = 4
    for r in range(0, rows0, chunk):
        qkv = project_rows(x0[r : r + chunk], mod0, qkv0, chunk, cols0, 0)
        q0[r : r + chunk] = (
            (qkv[:, :feat0].astype(BF16) * scale).astype(BF16).reshape(chunk, cols0, feat0)
        )
        store_kv(qkv[:, feat0:], k0, v0, HALO + r, chunk, cols0)
    halo_copies(n, me, x0, x0_halo, h0_send, h0_recv, rows0, "recv")
    for r, at in ((0, 0), (HALO, HALO + rows0)):
        kv = project_rows(x0_halo[r : r + HALO], mod0, qkv0, HALO, cols0, feat0)
        store_kv(kv, k0, v0, at, HALO, cols0)

    bias = window_bias(4)

    def fine(t, carry):
        c0 = pl.multiple_of(t * TILE, TILE)
        for r0 in range(0, rows0, 4):
            attend(q0, k0, v0, a0, bias, r0, c0, 0, 4, me * rows0, n * rows0, cols0)
        return carry

    lax.fori_loop(0, cols0 // TILE, fine, 0)
    loads[1].wait()
    loads[2].wait()
    y0 = gated(
        x0[...].reshape(rows0 * cols0, feat0), mod0, a0[...].reshape(rows0 * cols0, feat0), out0
    )
    x1[...] = merge(y0, merge0, rows0, cols0).reshape(rows1, cols1, feat1)

    halo_copies(n, me, x1, x1_halo, h1_send, h1_recv, rows1, "start")
    loads[3].wait()
    qkv = project_rows(x1[...], mod1, qkv1, rows1, cols1, 0)
    q1[...] = (qkv[:, :feat1].astype(BF16) * scale).astype(BF16).reshape(rows1, cols1, feat1)
    store_kv(qkv[:, feat1:], k1, v1, HALO, rows1, cols1)
    halo_copies(n, me, x1, x1_halo, h1_send, h1_recv, rows1, "recv")
    for r, at in ((0, 0), (HALO, HALO + rows1)):
        kv = project_rows(x1_halo[r : r + HALO], mod1, qkv1, HALO, cols1, feat1)
        store_kv(kv, k1, v1, at, HALO, cols1)

    def middle(t, carry):
        c0 = pl.multiple_of(t * TILE, TILE)
        for l0 in range(0, feat1, LANES):
            attend(q1, k1, v1, a1, bias, 0, c0, l0, rows1, me * rows1, n * rows1, cols1)
        return carry

    lax.fori_loop(0, cols1 // TILE, middle, 0)
    loads[4].wait()
    loads[5].wait()
    y1 = gated(
        x1[...].reshape(rows1 * cols1, feat1), mod1, a1[...].reshape(rows1 * cols1, feat1), out1
    )
    x2 = merge(y1, merge1, rows1, cols1)

    loads[6].wait()
    h2 = modulate(x2.astype(F32), mod2)
    inner = HEADS2 * DH
    qkv = dot(h2, qkv2[...])
    slot = lax.rem(me, HEADS2)
    base = me - slot
    blank = jnp.zeros((count2, DH), F32)
    for h in range(HEADS2):
        q = qkv[:, h * DH : (h + 1) * DH].astype(BF16).astype(F32) * scale
        k = qkv[:, inner + h * DH : inner + (h + 1) * DH]
        v = qkv[:, 2 * inner + h * DH : 2 * inner + (h + 1) * DH]
        q_out[h] = jnp.concatenate([q, blank], axis=1).astype(BF16)
        kv_out[h] = jnp.concatenate([k, v], axis=1).astype(BF16)

    def kv_copy(p):
        peer = lax.rem(me + p, n)
        return remote(
            kv_out.at[lax.rem(peer, HEADS2)], kv_all.at[me], kv_send.at[p], kv_recv.at[me], peer
        )

    def kv_from(p):
        peer = lax.rem(me + p, n)
        return remote(kv_out.at[0], kv_all.at[peer], kv_send.at[p], kv_recv.at[peer], peer)

    def q_copy(p):
        other = lax.rem(slot + p, HEADS2)
        return remote(
            q_out.at[other], q_all.at[slot], q_send.at[p], q_recv.at[slot], base + other
        )

    def q_from(p):
        other = lax.rem(slot + p, HEADS2)
        return remote(q_out.at[0], q_all.at[other], q_send.at[p], q_recv.at[other], base + other)

    def o_copy(p):
        other = lax.rem(slot + p, HEADS2)
        return remote(
            o_out.at[other], o_all.at[slot], o_send.at[p], o_recv.at[slot], base + other
        )

    def o_from(p):
        other = lax.rem(slot + p, HEADS2)
        return remote(o_out.at[0], o_all.at[other], o_send.at[p], o_recv.at[other], base + other)

    def each(count, make, act):
        def step(p, carry):
            act(make(p))
            return carry

        lax.fori_loop(1, count, step, 0)

    each(n, kv_copy, lambda c: c.start())
    each(HEADS2, q_copy, lambda c: c.start())
    kv_all[me] = kv_out[slot]
    q_all[slot] = q_out[slot]
    each(HEADS2, q_from, lambda c: c.wait_recv())
    each(n, kv_from, lambda c: c.wait_recv())

    piece = min(n, 16)
    queries = q_all[...].reshape(HEADS2 * count2, 2 * DH)
    block = 128

    def keys_step(t, carry):
        kv = kv_all[pl.ds(t * piece, piece)].reshape(piece * count2, 2 * DH)
        after = []
        for b, (top, total, summed) in enumerate(carry):
            s = dot_t(queries[b * block : (b + 1) * block], kv)
            new = jnp.maximum(top, jnp.max(s, axis=-1, keepdims=True))
            fade = jnp.exp(top - new)
            e = jnp.exp(s - new)
            after.append(
                (
                    new,
                    total * fade + jnp.sum(e, axis=-1, keepdims=True),
                    summed * fade + dot(e.astype(BF16), kv),
                )
            )
        return tuple(after)

    start = tuple(
        (
            jnp.full((block, 1), NEGATIVE, F32),
            jnp.zeros((block, 1), F32),
            jnp.zeros((block, 2 * DH), F32),
        )
        for _ in range(HEADS2 * count2 // block)
    )
    if n == piece:
        done = keys_step(0, start)
    else:
        done = lax.fori_loop(0, n // piece, keys_step, start)
    for b, (top, total, summed) in enumerate(done):
        per = block // count2
        o_out[b * per : (b + 1) * per] = (
            (summed / total).astype(BF16).reshape(per, count2, 2 * DH)
        )
    each(HEADS2, o_copy, lambda c: c.start())
    o_all[slot] = o_out[slot]
    loads[7].wait()
    each(HEADS2, o_from, lambda c: c.wait_recv())
    attended = jnp.concatenate([o_all[h].astype(F32)[:, DH:] for h in range(HEADS2)], axis=1)
    result[...] = gated(x2, mod2, attended.astype(BF16), out2).reshape(rows2, cols2, x2.shape[1])

    halo_copies(n, me, x0, x0_halo, h0_send, h0_recv, rows0, "send")
    halo_copies(n, me, x1, x1_halo, h1_send, h1_recv, rows1, "send")
    each(n, kv_copy, lambda c: c.wait_send())
    each(HEADS2, q_copy, lambda c: c.wait_send())
    each(HEADS2, o_copy, lambda c: c.wait_send())


def on_device(n, *args):
    tok, _, w_qkv0, w_out0, w_merge0, _, w_qkv1, w_out1, w_merge1, _, w_qkv2, w_out2 = args
    rows0, cols0, feat0 = tok.shape
    rows1, cols1, feat1 = rows0 // 2, cols0 // 2, w_merge0.shape[1]
    rows2, cols2, feat2 = rows1 // 2, cols1 // 2, w_merge1.shape[1]
    count2 = rows2 * cols2
    weights = [w_qkv0, w_out0, w_merge0, w_qkv1, w_out1, w_merge1, w_qkv2, w_out2]

    def vm(*shape):
        return pltpu.VMEM(shape, BF16)

    any_spec = pl.BlockSpec(memory_space=pl.ANY)
    vmem = pl.BlockSpec(memory_space=pltpu.VMEM)
    return pl.pallas_call(
        functools.partial(kernel, n),
        out_shape=jax.ShapeDtypeStruct((rows2, cols2, feat2), BF16),
        in_specs=[vmem if i in (1, 5, 9) else any_spec for i in range(12)],
        out_specs=vmem,
        scratch_shapes=[vm(*w.shape) for w in weights]
        + [pltpu.SemaphoreType.DMA((9,))]
        + [
            vm(rows0, cols0, feat0),
            vm(2 * HALO, cols0, feat0),
            vm(rows0, cols0, feat0),
            vm(rows0 + 2 * HALO, cols0 + 2 * PAD, feat0),
            vm(rows0 + 2 * HALO, cols0 + 2 * PAD, feat0),
            vm(rows0, cols0, feat0),
            vm(rows1, cols1, feat1),
            vm(2 * HALO, cols1, feat1),
            vm(rows1, cols1, feat1),
            vm(rows1 + 2 * HALO, cols1 + 2 * PAD, feat1),
            vm(rows1 + 2 * HALO, cols1 + 2 * PAD, feat1),
            vm(rows1, cols1, feat1),
            vm(HEADS2, count2, 2 * DH),
            vm(HEADS2, count2, 2 * DH),
            vm(HEADS2, count2, 2 * DH),
            vm(n, count2, 2 * DH),
            vm(HEADS2, count2, 2 * DH),
            vm(HEADS2, count2, 2 * DH),
        ]
        + [pltpu.SemaphoreType.DMA((2,))] * 4
        + [pltpu.SemaphoreType.DMA((n,))] * 2
        + [pltpu.SemaphoreType.DMA((HEADS2,))] * 4,
        compiler_params=pltpu.CompilerParams(
            collective_id=0, has_side_effects=True, vmem_limit_bytes=56 * 1024 * 1024
        ),
    )(*args)


def solution(mesh):
    return jax.shard_map(
        functools.partial(on_device, mesh.shape["row"]),
        mesh=mesh,
        in_specs=(
            P(("groups", "row"), None, None),
            P("groups", None),
            P(),
            P(),
            P(),
            P("groups", None),
            P(),
            P(),
            P(),
            P("groups", None),
            P(),
            P(),
        ),
        out_specs=P(("groups", "row"), None, None),
        check_vma=False,
    )
```

```python
import functools

import jax
import jax.numpy as jnp
from jax import lax
from jax.experimental import pallas as pl
from jax.experimental.pallas import tpu as pltpu
from jax.sharding import PartitionSpec as P

DH = 64
HEADS2 = 8
HALO = 3
PAD = 8
TILE = 32
SPAN = TILE + 2 * PAD
LANES = 256
EPSILON = 1e-06
NEGATIVE = -1e30
MESH = pl.DeviceIdType.MESH
F32 = jnp.float32
BF16 = jnp.bfloat16


def modulate(values, mod_ref):
    center = values - jnp.mean(values, axis=-1, keepdims=True)
    spread = jnp.mean(center * center, axis=-1, keepdims=True)
    normed = center * lax.rsqrt(spread + EPSILON)
    return (normed * (1.0 + mod_ref[1:2, :]) + mod_ref[0:1, :]).astype(BF16)


def dot(a, b):
    return jnp.dot(a, b, preferred_element_type=F32)


def dot_t(a, b):
    return lax.dot_general(a, b, (((1,), (1,)), ((), ())), preferred_element_type=F32)


def key_position(count):
    n = lax.broadcasted_iota(jnp.int32, (1, count), 1)
    row = jnp.zeros((1, count), jnp.int32)
    for step in range(1, count // SPAN):
        row = row + (n >= step * SPAN).astype(jnp.int32)
    return row, n - row * SPAN


def window_bias(rows):
    k_row, k_col = key_position((rows + 2 * HALO) * SPAN)
    m = lax.broadcasted_iota(jnp.int32, (rows * TILE, 1), 0)
    row_gap = k_row - m // TILE
    col_gap = k_col - PAD - m % TILE
    near = (row_gap >= 0) & (row_gap <= 2 * HALO) & (col_gap >= -HALO) & (col_gap <= HALO)
    return jnp.where(near, 0.0, NEGATIVE).astype(F32)


def project_rows(x, mod_ref, w_ref, row_count, col_count, first):
    h = modulate(x.reshape(row_count * col_count, x.shape[-1]).astype(F32), mod_ref)
    return dot(h, w_ref[:, first:])


def store_kv(kv, k_ref, v_ref, at, row_count, col_count):
    feat = kv.shape[1] // 2
    zero = jnp.zeros((row_count, PAD, 2 * feat), F32)
    kv = kv.reshape(row_count, col_count, 2 * feat)
    kv = jnp.concatenate([zero, kv, zero], axis=1).astype(BF16)
    k_ref[pl.ds(at, row_count)] = kv[:, :, :feat]
    v_ref[pl.ds(at, row_count)] = kv[:, :, feat:]


def attend(q_ref, k_ref, v_ref, o_ref, bias, r0, c0, l0, rows, row_start, total_rows, col_count):
    keys = (rows + 2 * HALO) * SPAN
    m = rows * TILE
    heads = LANES // DH
    lane_head = lax.broadcasted_iota(jnp.int32, (1, LANES), 1) // DH
    k_row, k_col = key_position(keys)
    g_row = row_start + r0 + k_row - HALO
    g_col = c0 + k_col - PAD
    inside = (g_row >= 0) & (g_row < total_rows) & (g_col >= 0) & (g_col < col_count)
    bias = bias + jnp.where(inside, 0.0, NEGATIVE).astype(F32)
    q = q_ref[pl.ds(r0, rows), pl.ds(c0, TILE), l0 : l0 + LANES].reshape(m, LANES)
    k = k_ref[pl.ds(r0, rows + 2 * HALO), pl.ds(c0, SPAN), l0 : l0 + LANES].reshape(keys, LANES)
    v = v_ref[pl.ds(r0, rows + 2 * HALO), pl.ds(c0, SPAN), l0 : l0 + LANES].reshape(keys, LANES)
    out = jnp.zeros((m, LANES), F32)
    stacked = jnp.concatenate(
        [q * (lane_head == h).astype(F32).astype(BF16) for h in range(heads)], axis=0
    )
    s = dot_t(stacked, k).reshape(heads, m, keys) + bias[None]
    top = jnp.max(s, axis=-1, keepdims=True)
    e = jnp.exp(s - top)
    total = jnp.sum(e, axis=-1, keepdims=True)
    o = dot(e.astype(BF16).reshape(heads * m, keys), v).reshape(heads, m, LANES) / total
    for h in range(heads):
        out = jnp.where(lane_head == h, o[h], out)
    o_ref[pl.ds(r0, rows), pl.ds(c0, TILE), l0 : l0 + LANES] = out.astype(BF16).reshape(
        rows, TILE, LANES
    )


def gated(x, mod_ref, attended, w_ref):
    return (x.astype(F32) + mod_ref[2:3, :] * dot(attended, w_ref[...])).astype(BF16)


def merge(y, w_ref, row_count, col_count):
    half = col_count // 2
    i = lax.broadcasted_iota(jnp.int32, (col_count, col_count), 0)
    j = lax.broadcasted_iota(jnp.int32, (col_count, col_count), 1)
    source = jnp.where(i < half, 2 * i, 2 * (i - half) + 1)
    pick = (source == j).astype(F32).astype(BF16)
    lines = []
    for r in range(0, row_count, 2):
        parts = []
        for u in (r, r + 1):
            both = dot(pick, y[u * col_count : (u + 1) * col_count]).astype(BF16)
            parts += [both[:half], both[half:]]
        lines.append(jnp.concatenate(parts, axis=1))
    return dot(jnp.concatenate(lines, axis=0), w_ref[...]).astype(BF16)


def remote(src, dst, send, recv, peer):
    return pltpu.make_async_remote_copy(
        src_ref=src, dst_ref=dst, send_sem=send, recv_sem=recv,
        device_id={"row": peer}, device_id_type=MESH,
    )


def halo_copies(n, me, src, dst, send, recv, down, up):
    below, above = jnp.minimum(me + 1, n - 1), jnp.maximum(me - 1, 0)
    made = []
    for i, (peer, (first, count, at)) in enumerate([(below, p) for p in down] + [(above, p) for p in up]):
        made.append(
            remote(
                src.at[pl.ds(first, count)], dst.at[pl.ds(at, count)], send.at[i], recv.at[i], peer
            )
        )
    return made[: len(down)], made[len(down) :]


def kernel(
    n,
    tok, mod0, w_qkv0, w_out0, w_merge0, mod1, w_qkv1, w_out1, w_merge1, mod2, w_qkv2, w_out2,
    result,
    qkv0, out0, merge0, qkv1, out1, merge1, qkv2, out2, w_sem,
    x0, x0_halo, q0, k0, v0, a0, x1, x1_halo, q1, k1, v1, a1,
    kv_out, q_out, o_out, kv_all, q_all, o_all,
    h0_send, h0_recv, h1_send, h1_recv, kv_send, kv_recv, q_send, q_recv, o_send, o_recv,
):
    rows0, cols0, feat0 = tok.shape
    rows1, cols1, feat1 = rows0 // 2, cols0 // 2, x1.shape[2]
    rows2, cols2 = rows1 // 2, cols1 // 2
    count2 = rows2 * cols2
    me = lax.axis_index("row")
    scale = DH**-0.5

    own = pltpu.make_async_copy(tok, x0, w_sem.at[8])
    own.start()
    loads = [
        pltpu.make_async_copy(src, dst, w_sem.at[i])
        for i, (src, dst) in enumerate(
            [(w_qkv0, qkv0), (w_out0, out0), (w_merge0, merge0), (w_qkv1, qkv1),
             (w_out1, out1), (w_merge1, merge1), (w_qkv2, qkv2), (w_out2, out2)]
        )
    ]
    loads[0].start()

    barrier = pltpu.get_barrier_semaphore()

    def greet(p, carry):
        pl.semaphore_signal(
            barrier, inc=1, device_id={"row": lax.rem(me + p, n)}, device_id_type=MESH
        )
        return carry

    lax.fori_loop(1, n, greet, 0)

    @pl.when(me == 0)
    def _():
        x0_halo[0:HALO] = jnp.zeros((HALO, cols0, feat0), BF16)
        x1_halo[0:HALO] = jnp.zeros((HALO, cols1, feat1), BF16)

    @pl.when(me == n - 1)
    def _():
        x0_halo[HALO:] = jnp.zeros((HALO, cols0, feat0), BF16)
        x1_halo[HALO:] = jnp.zeros((HALO, cols1, feat1), BF16)

    own.wait()
    pl.semaphore_wait(barrier, n - 1)
    has_below, has_above = me < n - 1, me > 0
    down0, up0 = halo_copies(
        n, me, x0, x0_halo, h0_send, h0_recv, [(rows0 - HALO, HALO, 0)], [(0, HALO, HALO)]
    )
    early, late = rows1 // 2, rows1 - HALO
    down1, up1 = halo_copies(
        n, me, x1, x1_halo, h1_send, h1_recv,
        [(late, early - late, 0), (early, rows1 - early, early - late)],
        [(0, early, HALO), (early, HALO - early, HALO + early)],
    )

    @pl.when(has_below)
    def _():
        down0[0].start()

    @pl.when(has_above)
    def _():
        up0[0].start()

    loads[0].wait()
    for load in loads[1:]:
        load.start()
    chunk = rows0 // 2
    for r in range(0, rows0, chunk):
        qkv = project_rows(x0[r : r + chunk], mod0, qkv0, chunk, cols0, 0)
        q0[r : r + chunk] = (
            (qkv[:, :feat0].astype(BF16) * scale).astype(BF16).reshape(chunk, cols0, feat0)
        )
        store_kv(qkv[:, feat0:], k0, v0, HALO + r, chunk, cols0)

    bias = window_bias(chunk)
    first = 1 - lax.rem(me, 2)
    for part in range(2):
        half = first if part == 0 else 1 - first
        r0 = half * chunk

        @pl.when(has_below & (half == 1))
        def _():
            up0[0].wait_recv()

        @pl.when(has_above & (half == 0))
        def _():
            down0[0].wait_recv()

        kv = project_rows(x0_halo[pl.ds(half * HALO, HALO)], mod0, qkv0, HALO, cols0, feat0)
        store_kv(kv, k0, v0, half * (HALO + rows0), HALO, cols0)

        def fine(t, carry):
            for u in range(2):
                c0 = pl.multiple_of(t * (2 * TILE) + u * TILE, TILE)
                attend(
                    q0, k0, v0, a0, bias, r0, c0, 0, chunk, me * rows0, n * rows0, cols0
                )
            return carry

        lax.fori_loop(0, cols0 // (2 * TILE), fine, 0)
        if part == 0:
            loads[1].wait()
            loads[2].wait()
        y0 = gated(
            x0[pl.ds(r0, chunk)].reshape(chunk * cols0, feat0), mod0,
            a0[pl.ds(r0, chunk)].reshape(chunk * cols0, feat0), out0,
        )
        x1[pl.ds(half * early, early)] = merge(y0, merge0, chunk, cols0).reshape(
            early, cols1, feat1
        )
        for side in range(2):

            @pl.when(has_below & (half == side))
            def _():
                down1[side].start()

            @pl.when(has_above & (half == side))
            def _():
                up1[side].start()

    loads[3].wait()
    qkv = project_rows(x1[...], mod1, qkv1, rows1, cols1, 0)
    q1[...] = (qkv[:, :feat1].astype(BF16) * scale).astype(BF16).reshape(rows1, cols1, feat1)
    store_kv(qkv[:, feat1:], k1, v1, HALO, rows1, cols1)

    @pl.when(has_above)
    def _():
        down1[0].wait_recv()
        down1[1].wait_recv()

    @pl.when(has_below)
    def _():
        up1[0].wait_recv()
        up1[1].wait_recv()

    for r, at in ((0, 0), (HALO, HALO + rows1)):
        kv = project_rows(x1_halo[r : r + HALO], mod1, qkv1, HALO, cols1, feat1)
        store_kv(kv, k1, v1, at, HALO, cols1)

    def middle(t, carry):
        c0 = pl.multiple_of(t * TILE, TILE)
        for l0 in range(0, feat1, LANES):
            attend(q1, k1, v1, a1, bias, 0, c0, l0, rows1, me * rows1, n * rows1, cols1)
        return carry

    lax.fori_loop(0, cols1 // TILE, middle, 0)
    loads[4].wait()
    loads[5].wait()
    y1 = gated(
        x1[...].reshape(rows1 * cols1, feat1), mod1, a1[...].reshape(rows1 * cols1, feat1), out1
    )
    x2 = merge(y1, merge1, rows1, cols1)

    loads[6].wait()
    h2 = modulate(x2.astype(F32), mod2)
    inner = HEADS2 * DH
    slot = lax.rem(me, HEADS2)
    base = me - slot
    blank = jnp.zeros((count2, DH), F32)
    kv = dot(h2, qkv2[:, inner:])
    for h in range(HEADS2):
        k = kv[:, h * DH : (h + 1) * DH]
        v = kv[:, inner + h * DH : inner + (h + 1) * DH]
        kv_out[h] = jnp.concatenate([k, v], axis=1).astype(BF16)

    def kv_copy(p):
        peer = lax.rem(me + p, n)
        return remote(
            kv_out.at[lax.rem(peer, HEADS2)], kv_all.at[me], kv_send.at[p], kv_recv.at[me], peer
        )

    def kv_from(p):
        peer = lax.rem(me + p, n)
        return remote(kv_out.at[0], kv_all.at[peer], kv_send.at[p], kv_recv.at[peer], peer)

    def q_copy(p):
        other = lax.rem(slot + p, HEADS2)
        return remote(
            q_out.at[other], q_all.at[slot], q_send.at[p], q_recv.at[slot], base + other
        )

    def q_from(p):
        other = lax.rem(slot + p, HEADS2)
        return remote(q_out.at[0], q_all.at[other], q_send.at[p], q_recv.at[other], base + other)

    def o_copy(other):
        return remote(
            o_out.at[other], o_all.at[slot], o_send.at[other], o_recv.at[slot], base + other
        )

    def o_from(p):
        other = lax.rem(slot + p, HEADS2)
        return remote(o_out.at[0], o_all.at[other], o_send.at[other], o_recv.at[other], base + other)

    def each(count, make, act):
        def step(p, carry):
            act(make(p))
            return carry

        lax.fori_loop(1, count, step, 0)

    each(n, kv_copy, lambda c: c.start())
    q = dot(h2, qkv2[:, :inner]).astype(BF16).astype(F32) * scale
    for h in range(HEADS2):
        q_out[h] = jnp.concatenate([q[:, h * DH : (h + 1) * DH], blank], axis=1).astype(BF16)
    each(HEADS2, q_copy, lambda c: c.start())
    kv_all[me] = kv_out[slot]
    q_all[slot] = q_out[slot]
    each(HEADS2, q_from, lambda c: c.wait_recv())
    each(n, kv_from, lambda c: c.wait_recv())

    piece = min(n, 16)
    queries = q_all[...].reshape(HEADS2 * count2, 2 * DH)
    block = 128

    for b in range(HEADS2 * count2 // block):
        asked = queries[b * block : (b + 1) * block]

        def keys_step(t, carry):
            top, total, summed = carry
            kv = kv_all[pl.ds(t * piece, piece)].reshape(piece * count2, 2 * DH)
            s = dot_t(asked, kv)
            new = jnp.maximum(top, jnp.max(s, axis=-1, keepdims=True))
            fade = jnp.exp(top - new)
            e = jnp.exp(s - new)
            return (
                new,
                total * fade + jnp.sum(e, axis=-1, keepdims=True),
                summed * fade + dot(e.astype(BF16), kv),
            )

        start = (
            jnp.full((block, 1), NEGATIVE, F32),
            jnp.zeros((block, 1), F32),
            jnp.zeros((block, 2 * DH), F32),
        )
        if n == piece:
            _, total, summed = keys_step(0, start)
        else:
            _, total, summed = lax.fori_loop(0, n // piece, keys_step, start)
        per = block // count2
        o_out[b * per : (b + 1) * per] = (
            (summed / total).astype(BF16).reshape(per, count2, 2 * DH)
        )
        for other in range(b * per, (b + 1) * per):

            @pl.when(other != slot)
            def _():
                o_copy(other).start()

    o_all[slot] = o_out[slot]
    loads[7].wait()
    each(HEADS2, o_from, lambda c: c.wait_recv())
    attended = jnp.concatenate([o_all[h].astype(F32)[:, DH:] for h in range(HEADS2)], axis=1)
    result[...] = gated(x2, mod2, attended.astype(BF16), out2).reshape(rows2, cols2, x2.shape[1])

    @pl.when(has_below)
    def _():
        for copy in (down0[0], down1[0], down1[1]):
            copy.wait_send()

    @pl.when(has_above)
    def _():
        for copy in (up0[0], up1[0], up1[1]):
            copy.wait_send()

    each(n, kv_copy, lambda c: c.wait_send())
    each(HEADS2, q_copy, lambda c: c.wait_send())
    each(HEADS2, o_from, lambda c: c.wait_send())


def on_device(n, *args):
    tok, _, w_qkv0, w_out0, w_merge0, _, w_qkv1, w_out1, w_merge1, _, w_qkv2, w_out2 = args
    rows0, cols0, feat0 = tok.shape
    rows1, cols1, feat1 = rows0 // 2, cols0 // 2, w_merge0.shape[1]
    rows2, cols2, feat2 = rows1 // 2, cols1 // 2, w_merge1.shape[1]
    count2 = rows2 * cols2
    weights = [w_qkv0, w_out0, w_merge0, w_qkv1, w_out1, w_merge1, w_qkv2, w_out2]

    def vm(*shape):
        return pltpu.VMEM(shape, BF16)

    any_spec = pl.BlockSpec(memory_space=pl.ANY)
    vmem = pl.BlockSpec(memory_space=pltpu.VMEM)
    return pl.pallas_call(
        functools.partial(kernel, n),
        out_shape=jax.ShapeDtypeStruct((rows2, cols2, feat2), BF16),
        in_specs=[vmem if i in (1, 5, 9) else any_spec for i in range(12)],
        out_specs=vmem,
        scratch_shapes=[vm(*w.shape) for w in weights]
        + [pltpu.SemaphoreType.DMA((9,))]
        + [
            vm(rows0, cols0, feat0),
            vm(2 * HALO, cols0, feat0),
            vm(rows0, cols0, feat0),
            vm(rows0 + 2 * HALO, cols0 + 2 * PAD, feat0),
            vm(rows0 + 2 * HALO, cols0 + 2 * PAD, feat0),
            vm(rows0, cols0, feat0),
            vm(rows1, cols1, feat1),
            vm(2 * HALO, cols1, feat1),
            vm(rows1, cols1, feat1),
            vm(rows1 + 2 * HALO, cols1 + 2 * PAD, feat1),
            vm(rows1 + 2 * HALO, cols1 + 2 * PAD, feat1),
            vm(rows1, cols1, feat1),
            vm(HEADS2, count2, 2 * DH),
            vm(HEADS2, count2, 2 * DH),
            vm(HEADS2, count2, 2 * DH),
            vm(n, count2, 2 * DH),
            vm(HEADS2, count2, 2 * DH),
            vm(HEADS2, count2, 2 * DH),
        ]
        + [pltpu.SemaphoreType.DMA((4,))] * 4
        + [pltpu.SemaphoreType.DMA((n,))] * 2
        + [pltpu.SemaphoreType.DMA((HEADS2,))] * 4,
        compiler_params=pltpu.CompilerParams(
            collective_id=0, has_side_effects=True, vmem_limit_bytes=56 * 1024 * 1024
        ),
    )(*args)


def solution(mesh):
    return jax.shard_map(
        functools.partial(on_device, mesh.shape["row"]),
        mesh=mesh,
        in_specs=(
            P(("groups", "row"), None, None),
            P("groups", None),
            P(),
            P(),
            P(),
            P("groups", None),
            P(),
            P(),
            P(),
            P("groups", None),
            P(),
            P(),
        ),
        out_specs=P(("groups", "row"), None, None),
        check_vma=False,
    )
```

```python
import functools

import jax
import jax.numpy as jnp
from jax import lax
from jax.experimental import pallas as pl
from jax.experimental.pallas import tpu as pltpu
from jax.sharding import PartitionSpec as P

DH = 64
HEADS2 = 8
HALO = 3
PAD = 8
TILE = 32
SPAN = TILE + 2 * PAD
LANES = 256
EPSILON = 1e-06
NEGATIVE = -1e30
MESH = pl.DeviceIdType.MESH
F32 = jnp.float32
BF16 = jnp.bfloat16


def modulate(values, mod_ref):
    center = values - jnp.mean(values, axis=-1, keepdims=True)
    spread = jnp.mean(center * center, axis=-1, keepdims=True)
    normed = center * lax.rsqrt(spread + EPSILON)
    return (normed * (1.0 + mod_ref[1:2, :]) + mod_ref[0:1, :]).astype(BF16)


def dot(a, b):
    return jnp.dot(a, b, preferred_element_type=F32)


def dot_t(a, b):
    return lax.dot_general(a, b, (((1,), (1,)), ((), ())), preferred_element_type=F32)


def key_position(count):
    n = lax.broadcasted_iota(jnp.int32, (1, count), 1)
    row = jnp.zeros((1, count), jnp.int32)
    for step in range(1, count // SPAN):
        row = row + (n >= step * SPAN).astype(jnp.int32)
    return row, n - row * SPAN


def window_bias(rows):
    k_row, k_col = key_position((rows + 2 * HALO) * SPAN)
    m = lax.broadcasted_iota(jnp.int32, (rows * TILE, 1), 0)
    row_gap = k_row - m // TILE
    col_gap = k_col - PAD - m % TILE
    near = (row_gap >= 0) & (row_gap <= 2 * HALO) & (col_gap >= -HALO) & (col_gap <= HALO)
    return jnp.where(near, 0.0, NEGATIVE).astype(F32)


def project_rows(x, mod_ref, w_ref, row_count, col_count, first):
    h = modulate(x.reshape(row_count * col_count, x.shape[-1]).astype(F32), mod_ref)
    return dot(h, w_ref[:, first:])


def store_kv(kv, k_ref, v_ref, at, row_count, col_count):
    feat = kv.shape[1] // 2
    zero = jnp.zeros((row_count, PAD, 2 * feat), F32)
    kv = kv.reshape(row_count, col_count, 2 * feat)
    kv = jnp.concatenate([zero, kv, zero], axis=1).astype(BF16)
    k_ref[pl.ds(at, row_count)] = kv[:, :, :feat]
    v_ref[pl.ds(at, row_count)] = kv[:, :, feat:]


def attend(q_ref, k_ref, v_ref, o_ref, bias, r0, c0, l0, rows, row_start, total_rows, col_count):
    keys = (rows + 2 * HALO) * SPAN
    m = rows * TILE
    heads = LANES // DH
    lane_head = lax.broadcasted_iota(jnp.int32, (1, LANES), 1) // DH
    k_row, k_col = key_position(keys)
    g_row = row_start + r0 + k_row - HALO
    g_col = c0 + k_col - PAD
    inside = (g_row >= 0) & (g_row < total_rows) & (g_col >= 0) & (g_col < col_count)
    bias = bias + jnp.where(inside, 0.0, NEGATIVE).astype(F32)
    q = q_ref[pl.ds(r0, rows), pl.ds(c0, TILE), l0 : l0 + LANES].reshape(m, LANES)
    k = k_ref[pl.ds(r0, rows + 2 * HALO), pl.ds(c0, SPAN), l0 : l0 + LANES].reshape(keys, LANES)
    v = v_ref[pl.ds(r0, rows + 2 * HALO), pl.ds(c0, SPAN), l0 : l0 + LANES].reshape(keys, LANES)
    out = jnp.zeros((m, LANES), F32)
    stacked = jnp.concatenate(
        [q * (lane_head == h).astype(F32).astype(BF16) for h in range(heads)], axis=0
    )
    s = dot_t(stacked, k).reshape(heads, m, keys) + bias[None]
    top = jnp.max(s, axis=-1, keepdims=True)
    e = jnp.exp(s - top)
    total = jnp.sum(e, axis=-1, keepdims=True)
    o = dot(e.astype(BF16).reshape(heads * m, keys), v).reshape(heads, m, LANES) / total
    for h in range(heads):
        out = jnp.where(lane_head == h, o[h], out)
    o_ref[pl.ds(r0, rows), pl.ds(c0, TILE), l0 : l0 + LANES] = out.astype(BF16).reshape(
        rows, TILE, LANES
    )


def gated(x, mod_ref, attended, w_ref):
    return (x.astype(F32) + mod_ref[2:3, :] * dot(attended, w_ref[...])).astype(BF16)


def merge(y, w_ref, row_count, col_count):
    half = col_count // 2
    i = lax.broadcasted_iota(jnp.int32, (col_count, col_count), 0)
    j = lax.broadcasted_iota(jnp.int32, (col_count, col_count), 1)
    source = jnp.where(i < half, 2 * i, 2 * (i - half) + 1)
    pick = (source == j).astype(F32).astype(BF16)
    lines = []
    for r in range(0, row_count, 2):
        parts = []
        for u in (r, r + 1):
            both = dot(pick, y[u * col_count : (u + 1) * col_count]).astype(BF16)
            parts += [both[:half], both[half:]]
        lines.append(jnp.concatenate(parts, axis=1))
    return dot(jnp.concatenate(lines, axis=0), w_ref[...]).astype(BF16)


def remote(src, dst, send, recv, peer):
    return pltpu.make_async_remote_copy(
        src_ref=src, dst_ref=dst, send_sem=send, recv_sem=recv,
        device_id={"row": peer}, device_id_type=MESH,
    )


def halo_copies(n, me, src, dst, send, recv, down, up):
    below, above = jnp.minimum(me + 1, n - 1), jnp.maximum(me - 1, 0)
    made = []
    for i, (peer, (first, count, at)) in enumerate([(below, p) for p in down] + [(above, p) for p in up]):
        made.append(
            remote(
                src.at[pl.ds(first, count)], dst.at[pl.ds(at, count)], send.at[i], recv.at[i], peer
            )
        )
    return made[: len(down)], made[len(down) :]


def kernel(
    n,
    tok, mod0, w_qkv0, w_out0, w_merge0, mod1, w_qkv1, w_out1, w_merge1, mod2, w_qkv2, w_out2,
    result,
    qkv0, out0, merge0, qkv1, out1, merge1, qkv2, out2, w_sem,
    x0, x0_halo, q0, k0, v0, a0, x1, x1_halo, q1, k1, v1, a1,
    kv_out, q_out, o_out, kv_all, q_all, o_all,
    h0_send, h0_recv, h1_send, h1_recv, kv_send, kv_recv, q_send, q_recv, o_send, o_recv,
):
    rows0, cols0, feat0 = tok.shape
    rows1, cols1, feat1 = rows0 // 2, cols0 // 2, x1.shape[2]
    rows2, cols2 = rows1 // 2, cols1 // 2
    count2 = rows2 * cols2
    me = lax.axis_index("row")
    scale = DH**-0.5

    own = pltpu.make_async_copy(tok, x0, w_sem.at[8])
    own.start()
    loads = [
        pltpu.make_async_copy(src, dst, w_sem.at[i])
        for i, (src, dst) in enumerate(
            [(w_qkv0, qkv0), (w_out0, out0), (w_merge0, merge0), (w_qkv1, qkv1),
             (w_out1, out1), (w_merge1, merge1), (w_qkv2, qkv2), (w_out2, out2)]
        )
    ]
    loads[0].start()

    barrier = pltpu.get_barrier_semaphore()

    def greet(p, carry):
        pl.semaphore_signal(
            barrier, inc=1, device_id={"row": lax.rem(me + p, n)}, device_id_type=MESH
        )
        return carry

    lax.fori_loop(1, n, greet, 0)

    @pl.when(me == 0)
    def _():
        x0_halo[0:HALO] = jnp.zeros((HALO, cols0, feat0), BF16)
        x1_halo[0:HALO] = jnp.zeros((HALO, cols1, feat1), BF16)

    @pl.when(me == n - 1)
    def _():
        x0_halo[HALO:] = jnp.zeros((HALO, cols0, feat0), BF16)
        x1_halo[HALO:] = jnp.zeros((HALO, cols1, feat1), BF16)

    own.wait()
    pl.semaphore_wait(barrier, n - 1)
    has_below, has_above = me < n - 1, me > 0
    down0, up0 = halo_copies(
        n, me, x0, x0_halo, h0_send, h0_recv, [(rows0 - HALO, HALO, 0)], [(0, HALO, HALO)]
    )
    early, late = rows1 // 2, rows1 - HALO
    down1, up1 = halo_copies(
        n, me, x1, x1_halo, h1_send, h1_recv,
        [(late, early - late, 0), (early, rows1 - early, early - late)],
        [(0, early, HALO), (early, HALO - early, HALO + early)],
    )

    @pl.when(has_below)
    def _():
        down0[0].start()

    @pl.when(has_above)
    def _():
        up0[0].start()

    loads[0].wait()
    for load in loads[1:]:
        load.start()
    chunk = rows0 // 2
    for r in range(0, rows0, chunk):
        qkv = project_rows(x0[r : r + chunk], mod0, qkv0, chunk, cols0, 0)
        q0[r : r + chunk] = (
            (qkv[:, :feat0].astype(BF16) * scale).astype(BF16).reshape(chunk, cols0, feat0)
        )
        store_kv(qkv[:, feat0:], k0, v0, HALO + r, chunk, cols0)

    bias = window_bias(chunk)
    first = 1 - lax.rem(me, 2)
    for part in range(2):
        half = first if part == 0 else 1 - first
        r0 = half * chunk

        @pl.when(has_below & (half == 1))
        def _():
            up0[0].wait_recv()

        @pl.when(has_above & (half == 0))
        def _():
            down0[0].wait_recv()

        kv = project_rows(x0_halo[pl.ds(half * HALO, HALO)], mod0, qkv0, HALO, cols0, feat0)
        store_kv(kv, k0, v0, half * (HALO + rows0), HALO, cols0)

        def fine(t, carry):
            for u in range(2):
                c0 = pl.multiple_of(t * (2 * TILE) + u * TILE, TILE)
                attend(
                    q0, k0, v0, a0, bias, r0, c0, 0, chunk, me * rows0, n * rows0, cols0
                )
            return carry

        lax.fori_loop(0, cols0 // (2 * TILE), fine, 0)
        if part == 0:
            loads[1].wait()
            loads[2].wait()
        y0 = gated(
            x0[pl.ds(r0, chunk)].reshape(chunk * cols0, feat0), mod0,
            a0[pl.ds(r0, chunk)].reshape(chunk * cols0, feat0), out0,
        )
        x1[pl.ds(half * early, early)] = merge(y0, merge0, chunk, cols0).reshape(
            early, cols1, feat1
        )
        for side in range(2):

            @pl.when(has_below & (half == side))
            def _():
                down1[side].start()

            @pl.when(has_above & (half == side))
            def _():
                up1[side].start()

    loads[3].wait()
    qkv = project_rows(x1[...], mod1, qkv1, rows1, cols1, 0)
    q1[...] = (qkv[:, :feat1].astype(BF16) * scale).astype(BF16).reshape(rows1, cols1, feat1)
    store_kv(qkv[:, feat1:], k1, v1, HALO, rows1, cols1)

    @pl.when(has_above)
    def _():
        down1[0].wait_recv()
        down1[1].wait_recv()

    @pl.when(has_below)
    def _():
        up1[0].wait_recv()
        up1[1].wait_recv()

    kv = project_rows(x1_halo[...], mod1, qkv1, 2 * HALO, cols1, feat1)
    store_kv(kv[: HALO * cols1], k1, v1, 0, HALO, cols1)
    store_kv(kv[HALO * cols1 :], k1, v1, HALO + rows1, HALO, cols1)

    def middle(t, carry):
        c0 = pl.multiple_of(t * TILE, TILE)
        for l0 in range(0, feat1, LANES):
            attend(q1, k1, v1, a1, bias, 0, c0, l0, rows1, me * rows1, n * rows1, cols1)
        return carry

    lax.fori_loop(0, cols1 // TILE, middle, 0)
    loads[4].wait()
    loads[5].wait()
    y1 = gated(
        x1[...].reshape(rows1 * cols1, feat1), mod1, a1[...].reshape(rows1 * cols1, feat1), out1
    )
    x2 = merge(y1, merge1, rows1, cols1)

    loads[6].wait()
    h2 = modulate(x2.astype(F32), mod2)
    inner = HEADS2 * DH
    slot = lax.rem(me, HEADS2)
    base = me - slot
    pair = count2 // 2
    kv = dot(h2, qkv2[:, inner:])
    for h in range(HEADS2):
        k = kv[:, h * DH : (h + 1) * DH]
        v = kv[:, inner + h * DH : inner + (h + 1) * DH]
        kv_out[h] = jnp.concatenate([k, v], axis=1).astype(BF16)

    def kv_copy(p):
        peer = lax.rem(me + p, n)
        return remote(
            kv_out.at[lax.rem(peer, HEADS2)], kv_all.at[me], kv_send.at[p], kv_recv.at[me], peer
        )

    def kv_from(p):
        peer = lax.rem(me + p, n)
        return remote(kv_out.at[0], kv_all.at[peer], kv_send.at[p], kv_recv.at[peer], peer)

    def q_copy(p):
        other = lax.rem(slot + p, HEADS2)
        return remote(
            q_out.at[other], q_all.at[slot], q_send.at[p], q_recv.at[slot], base + other
        )

    def q_from(p):
        other = lax.rem(slot + p, HEADS2)
        return remote(q_out.at[0], q_all.at[other], q_send.at[p], q_recv.at[other], base + other)

    def o_copy(other):
        return remote(
            o_out.at[other], o_all.at[slot], o_send.at[other], o_recv.at[slot], base + other
        )

    def o_from(p):
        other = lax.rem(slot + p, HEADS2)
        return remote(o_out.at[0], o_all.at[other], o_send.at[other], o_recv.at[other], base + other)

    def each(count, make, act):
        def step(p, carry):
            act(make(p))
            return carry

        lax.fori_loop(1, count, step, 0)


    def far_first(i, carry):
        p = lax.rem(i + n // 2 - HEADS2 // 2, n)

        @pl.when(p > 0)
        def _():
            kv_copy(p).start()

        return carry

    lax.fori_loop(0, n, far_first, 0)
    q = dot(h2, qkv2[:, :inner]).astype(BF16).astype(F32) * scale
    for h in range(HEADS2):
        mine = q[:, h * DH : (h + 1) * DH]
        q_out[h] = jnp.concatenate([mine[:pair], mine[pair:]], axis=1).astype(BF16)
    each(HEADS2, q_copy, lambda c: c.start())
    kv_all[me] = kv_out[slot]
    q_all[slot] = q_out[slot]
    each(HEADS2, q_from, lambda c: c.wait_recv())
    each(n, kv_from, lambda c: c.wait_recv())

    piece = min(n, 16)
    packed = q_all[...].astype(F32)
    blank = jnp.zeros((HEADS2, pair, DH), F32)
    queries = jnp.concatenate(
        [
            jnp.concatenate([packed[:, :, :DH], blank], axis=2),
            jnp.concatenate([packed[:, :, DH:], blank], axis=2),
        ],
        axis=1,
    )
    queries = queries.astype(BF16).reshape(HEADS2 * count2, 2 * DH)
    block = 128

    for b in range(HEADS2 * count2 // block):
        asked = queries[b * block : (b + 1) * block]

        def keys_step(t, carry):
            top, total, summed = carry
            kv = kv_all[pl.ds(t * piece, piece)].reshape(piece * count2, 2 * DH)
            s = dot_t(asked, kv)
            new = jnp.maximum(top, jnp.max(s, axis=-1, keepdims=True))
            fade = jnp.exp(top - new)
            e = jnp.exp(s - new)
            return (
                new,
                total * fade + jnp.sum(e, axis=-1, keepdims=True),
                summed * fade + dot(e.astype(BF16), kv),
            )

        start = (
            jnp.full((block, 1), NEGATIVE, F32),
            jnp.zeros((block, 1), F32),
            jnp.zeros((block, 2 * DH), F32),
        )
        if n == piece:
            _, total, summed = keys_step(0, start)
        else:
            _, total, summed = lax.fori_loop(0, n // piece, keys_step, start)
        per = block // count2
        o = (summed / total).reshape(per, count2, 2 * DH)
        o_out[b * per : (b + 1) * per] = jnp.concatenate(
            [o[:, :pair, DH:], o[:, pair:, DH:]], axis=2
        ).astype(BF16)
        for other in range(b * per, (b + 1) * per):

            @pl.when(other != slot)
            def _():
                o_copy(other).start()

    o_all[slot] = o_out[slot]
    loads[7].wait()
    each(HEADS2, o_from, lambda c: c.wait_recv())
    packed = o_all[...].astype(F32)
    attended = jnp.concatenate(
        [
            jnp.concatenate([packed[h, :, :DH], packed[h, :, DH:]], axis=0)
            for h in range(HEADS2)
        ],
        axis=1,
    )
    result[...] = gated(x2, mod2, attended.astype(BF16), out2).reshape(rows2, cols2, x2.shape[1])

    @pl.when(has_below)
    def _():
        for copy in (down0[0], down1[0], down1[1]):
            copy.wait_send()

    @pl.when(has_above)
    def _():
        for copy in (up0[0], up1[0], up1[1]):
            copy.wait_send()

    each(n, kv_copy, lambda c: c.wait_send())
    each(HEADS2, q_copy, lambda c: c.wait_send())
    each(HEADS2, o_from, lambda c: c.wait_send())


def on_device(n, *args):
    tok, _, w_qkv0, w_out0, w_merge0, _, w_qkv1, w_out1, w_merge1, _, w_qkv2, w_out2 = args
    rows0, cols0, feat0 = tok.shape
    rows1, cols1, feat1 = rows0 // 2, cols0 // 2, w_merge0.shape[1]
    rows2, cols2, feat2 = rows1 // 2, cols1 // 2, w_merge1.shape[1]
    count2 = rows2 * cols2
    weights = [w_qkv0, w_out0, w_merge0, w_qkv1, w_out1, w_merge1, w_qkv2, w_out2]

    def vm(*shape):
        return pltpu.VMEM(shape, BF16)

    any_spec = pl.BlockSpec(memory_space=pl.ANY)
    vmem = pl.BlockSpec(memory_space=pltpu.VMEM)
    return pl.pallas_call(
        functools.partial(kernel, n),
        out_shape=jax.ShapeDtypeStruct((rows2, cols2, feat2), BF16),
        in_specs=[vmem if i in (1, 5, 9) else any_spec for i in range(12)],
        out_specs=vmem,
        scratch_shapes=[vm(*w.shape) for w in weights]
        + [pltpu.SemaphoreType.DMA((9,))]
        + [
            vm(rows0, cols0, feat0),
            vm(2 * HALO, cols0, feat0),
            vm(rows0, cols0, feat0),
            vm(rows0 + 2 * HALO, cols0 + 2 * PAD, feat0),
            vm(rows0 + 2 * HALO, cols0 + 2 * PAD, feat0),
            vm(rows0, cols0, feat0),
            vm(rows1, cols1, feat1),
            vm(2 * HALO, cols1, feat1),
            vm(rows1, cols1, feat1),
            vm(rows1 + 2 * HALO, cols1 + 2 * PAD, feat1),
            vm(rows1 + 2 * HALO, cols1 + 2 * PAD, feat1),
            vm(rows1, cols1, feat1),
            vm(HEADS2, count2, 2 * DH),
            vm(HEADS2, count2 // 2, 2 * DH),
            vm(HEADS2, count2 // 2, 2 * DH),
            vm(n, count2, 2 * DH),
            vm(HEADS2, count2 // 2, 2 * DH),
            vm(HEADS2, count2 // 2, 2 * DH),
        ]
        + [pltpu.SemaphoreType.DMA((4,))] * 4
        + [pltpu.SemaphoreType.DMA((n,))] * 2
        + [pltpu.SemaphoreType.DMA((HEADS2,))] * 4,
        compiler_params=pltpu.CompilerParams(
            collective_id=0, has_side_effects=True, vmem_limit_bytes=56 * 1024 * 1024
        ),
    )(*args)


def solution(mesh):
    return jax.shard_map(
        functools.partial(on_device, mesh.shape["row"]),
        mesh=mesh,
        in_specs=(
            P(("groups", "row"), None, None),
            P("groups", None),
            P(),
            P(),
            P(),
            P("groups", None),
            P(),
            P(),
            P(),
            P("groups", None),
            P(),
            P(),
        ),
        out_specs=P(("groups", "row"), None, None),
        check_vma=False,
    )
```

```python
import functools

import jax
import jax.numpy as jnp
from jax import lax
from jax.experimental import pallas as pl
from jax.experimental.pallas import tpu as pltpu
from jax.sharding import PartitionSpec as P

DH = 64
HEADS2 = 8
HALO = 3
PAD = 8
TILE = 32
SPAN = TILE + 2 * PAD
LANES = 256
EPSILON = 1e-06
NEGATIVE = -1e30
MESH = pl.DeviceIdType.MESH
F32 = jnp.float32
BF16 = jnp.bfloat16


def modulate(values, mod_ref):
    center = values - jnp.mean(values, axis=-1, keepdims=True)
    spread = jnp.mean(center * center, axis=-1, keepdims=True)
    normed = center * lax.rsqrt(spread + EPSILON)
    return (normed * (1.0 + mod_ref[1:2, :]) + mod_ref[0:1, :]).astype(BF16)


def dot(a, b):
    return jnp.dot(a, b, preferred_element_type=F32)


def dot_t(a, b):
    return lax.dot_general(a, b, (((1,), (1,)), ((), ())), preferred_element_type=F32)


def key_position(count):
    n = lax.broadcasted_iota(jnp.int32, (1, count), 1)
    row = jnp.zeros((1, count), jnp.int32)
    for step in range(1, count // SPAN):
        row = row + (n >= step * SPAN).astype(jnp.int32)
    return row, n - row * SPAN


def window_bias(rows):
    k_row, k_col = key_position((rows + 2 * HALO) * SPAN)
    m = lax.broadcasted_iota(jnp.int32, (rows * TILE, 1), 0)
    row_gap = k_row - m // TILE
    col_gap = k_col - PAD - m % TILE
    near = (row_gap >= 0) & (row_gap <= 2 * HALO) & (col_gap >= -HALO) & (col_gap <= HALO)
    return jnp.where(near, 0.0, NEGATIVE).astype(F32)


def project_rows(x, mod_ref, w_ref, row_count, col_count, first):
    h = modulate(x.reshape(row_count * col_count, x.shape[-1]).astype(F32), mod_ref)
    return dot(h, w_ref[:, first:])


def store_kv(kv, k_ref, v_ref, at, row_count, col_count):
    feat = kv.shape[1] // 2
    zero = jnp.zeros((row_count, PAD, 2 * feat), F32)
    kv = kv.reshape(row_count, col_count, 2 * feat)
    kv = jnp.concatenate([zero, kv, zero], axis=1).astype(BF16)
    k_ref[pl.ds(at, row_count)] = kv[:, :, :feat]
    v_ref[pl.ds(at, row_count)] = kv[:, :, feat:]


def attend(q_ref, k_ref, v_ref, o_ref, bias, r0, c0, l0, rows, row_start, total_rows, col_count):
    keys = (rows + 2 * HALO) * SPAN
    m = rows * TILE
    heads = LANES // DH
    lane_head = lax.broadcasted_iota(jnp.int32, (1, LANES), 1) // DH
    k_row, k_col = key_position(keys)
    g_row = row_start + r0 + k_row - HALO
    g_col = c0 + k_col - PAD
    inside = (g_row >= 0) & (g_row < total_rows) & (g_col >= 0) & (g_col < col_count)
    bias = bias + jnp.where(inside, 0.0, NEGATIVE).astype(F32)
    q = q_ref[pl.ds(r0, rows), pl.ds(c0, TILE), l0 : l0 + LANES].reshape(m, LANES)
    k = k_ref[pl.ds(r0, rows + 2 * HALO), pl.ds(c0, SPAN), l0 : l0 + LANES].reshape(keys, LANES)
    v = v_ref[pl.ds(r0, rows + 2 * HALO), pl.ds(c0, SPAN), l0 : l0 + LANES].reshape(keys, LANES)
    out = jnp.zeros((m, LANES), F32)
    stacked = jnp.concatenate(
        [q * (lane_head == h).astype(F32).astype(BF16) for h in range(heads)], axis=0
    )
    s = dot_t(stacked, k).reshape(heads, m, keys) + bias[None]
    top = jnp.max(s, axis=-1, keepdims=True)
    e = jnp.exp(s - top)
    total = jnp.sum(e, axis=-1, keepdims=True)
    share = 1.0 / total
    o = dot(e.astype(BF16).reshape(heads * m, keys), v).reshape(heads, m, LANES)
    for h in range(heads):
        out = jnp.where(lane_head == h, o[h] * share[h], out)
    o_ref[pl.ds(r0, rows), pl.ds(c0, TILE), l0 : l0 + LANES] = out.astype(BF16).reshape(
        rows, TILE, LANES
    )


def gated(x, mod_ref, attended, w_ref):
    return (x.astype(F32) + mod_ref[2:3, :] * dot(attended, w_ref[...])).astype(BF16)


def merge(y, w_ref, row_count, col_count):
    half = col_count // 2
    i = lax.broadcasted_iota(jnp.int32, (col_count, col_count), 0)
    j = lax.broadcasted_iota(jnp.int32, (col_count, col_count), 1)
    source = jnp.where(i < half, 2 * i, 2 * (i - half) + 1)
    pick = (source == j).astype(F32).astype(BF16)
    lines = []
    for r in range(0, row_count, 2):
        parts = []
        for u in (r, r + 1):
            both = dot(pick, y[u * col_count : (u + 1) * col_count]).astype(BF16)
            parts += [both[:half], both[half:]]
        lines.append(jnp.concatenate(parts, axis=1))
    return dot(jnp.concatenate(lines, axis=0), w_ref[...]).astype(BF16)


def remote(src, dst, send, recv, peer):
    return pltpu.make_async_remote_copy(
        src_ref=src, dst_ref=dst, send_sem=send, recv_sem=recv,
        device_id={"row": peer}, device_id_type=MESH,
    )


def halo_copies(n, me, src, dst, send, recv, down, up):
    below, above = jnp.minimum(me + 1, n - 1), jnp.maximum(me - 1, 0)
    made = []
    for i, (peer, (first, count, at)) in enumerate([(below, p) for p in down] + [(above, p) for p in up]):
        made.append(
            remote(
                src.at[pl.ds(first, count)], dst.at[pl.ds(at, count)], send.at[i], recv.at[i], peer
            )
        )
    return made[: len(down)], made[len(down) :]


def kernel(
    n,
    tok, mod0, w_qkv0, w_out0, w_merge0, mod1, w_qkv1, w_out1, w_merge1, mod2, w_qkv2, w_out2,
    result,
    qkv0, out0, merge0, qkv1, out1, merge1, qkv2, out2, w_sem,
    x0, x0_halo, q0, k0, v0, a0, x1, x1_halo, q1, k1, v1, a1,
    kv_out, q_out, o_out, kv_all, q_all, o_all,
    h0_send, h0_recv, h1_send, h1_recv, kv_send, kv_recv, q_send, q_recv, o_send, o_recv,
):
    rows0, cols0, feat0 = tok.shape
    rows1, cols1, feat1 = rows0 // 2, cols0 // 2, x1.shape[2]
    rows2, cols2 = rows1 // 2, cols1 // 2
    count2 = rows2 * cols2
    me = lax.axis_index("row")
    scale = DH**-0.5

    own = pltpu.make_async_copy(tok, x0, w_sem.at[8])
    own.start()
    loads = [
        pltpu.make_async_copy(src, dst, w_sem.at[i])
        for i, (src, dst) in enumerate(
            [(w_qkv0, qkv0), (w_out0, out0), (w_merge0, merge0), (w_qkv1, qkv1),
             (w_out1, out1), (w_merge1, merge1), (w_qkv2, qkv2), (w_out2, out2)]
        )
    ]
    loads[0].start()

    barrier = pltpu.get_barrier_semaphore()

    def greet(p, carry):
        pl.semaphore_signal(
            barrier, inc=1, device_id={"row": lax.rem(me + p, n)}, device_id_type=MESH
        )
        return carry

    lax.fori_loop(1, n, greet, 0)

    @pl.when(me == 0)
    def _():
        x0_halo[0:HALO] = jnp.zeros((HALO, cols0, feat0), BF16)
        x1_halo[0:HALO] = jnp.zeros((HALO, cols1, feat1), BF16)

    @pl.when(me == n - 1)
    def _():
        x0_halo[HALO:] = jnp.zeros((HALO, cols0, feat0), BF16)
        x1_halo[HALO:] = jnp.zeros((HALO, cols1, feat1), BF16)

    own.wait()
    pl.semaphore_wait(barrier, n - 1)
    has_below, has_above = me < n - 1, me > 0
    down0, up0 = halo_copies(
        n, me, x0, x0_halo, h0_send, h0_recv, [(rows0 - HALO, HALO, 0)], [(0, HALO, HALO)]
    )
    early, late = rows1 // 2, rows1 - HALO
    down1, up1 = halo_copies(
        n, me, x1, x1_halo, h1_send, h1_recv,
        [(late, early - late, 0), (early, rows1 - early, early - late)],
        [(0, early, HALO), (early, HALO - early, HALO + early)],
    )

    @pl.when(has_below)
    def _():
        down0[0].start()

    @pl.when(has_above)
    def _():
        up0[0].start()

    loads[0].wait()
    for load in loads[1:]:
        load.start()
    chunk = rows0 // 2
    for r in range(0, rows0, chunk):
        qkv = project_rows(x0[r : r + chunk], mod0, qkv0, chunk, cols0, 0)
        q0[r : r + chunk] = (
            (qkv[:, :feat0].astype(BF16) * scale).astype(BF16).reshape(chunk, cols0, feat0)
        )
        store_kv(qkv[:, feat0:], k0, v0, HALO + r, chunk, cols0)

    bias = window_bias(chunk)
    first = 1 - lax.rem(me, 2)
    for part in range(2):
        half = first if part == 0 else 1 - first
        r0 = half * chunk

        @pl.when(has_below & (half == 1))
        def _():
            up0[0].wait_recv()

        @pl.when(has_above & (half == 0))
        def _():
            down0[0].wait_recv()

        kv = project_rows(x0_halo[pl.ds(half * HALO, HALO)], mod0, qkv0, HALO, cols0, feat0)
        store_kv(kv, k0, v0, half * (HALO + rows0), HALO, cols0)

        def fine(t, carry):
            for u in range(2):
                c0 = pl.multiple_of(t * (2 * TILE) + u * TILE, TILE)
                attend(
                    q0, k0, v0, a0, bias, r0, c0, 0, chunk, me * rows0, n * rows0, cols0
                )
            return carry

        lax.fori_loop(0, cols0 // (2 * TILE), fine, 0)
        if part == 0:
            loads[1].wait()
            loads[2].wait()
        y0 = gated(
            x0[pl.ds(r0, chunk)].reshape(chunk * cols0, feat0), mod0,
            a0[pl.ds(r0, chunk)].reshape(chunk * cols0, feat0), out0,
        )
        x1[pl.ds(half * early, early)] = merge(y0, merge0, chunk, cols0).reshape(
            early, cols1, feat1
        )
        for side in range(2):

            @pl.when(has_below & (half == side))
            def _():
                down1[side].start()

            @pl.when(has_above & (half == side))
            def _():
                up1[side].start()

    loads[3].wait()
    qkv = project_rows(x1[...], mod1, qkv1, rows1, cols1, 0)
    q1[...] = (qkv[:, :feat1].astype(BF16) * scale).astype(BF16).reshape(rows1, cols1, feat1)
    store_kv(qkv[:, feat1:], k1, v1, HALO, rows1, cols1)

    @pl.when(has_above)
    def _():
        down1[0].wait_recv()
        down1[1].wait_recv()

    @pl.when(has_below)
    def _():
        up1[0].wait_recv()
        up1[1].wait_recv()

    kv = project_rows(x1_halo[...], mod1, qkv1, 2 * HALO, cols1, feat1)
    store_kv(kv[: HALO * cols1], k1, v1, 0, HALO, cols1)
    store_kv(kv[HALO * cols1 :], k1, v1, HALO + rows1, HALO, cols1)

    for c0 in range(0, cols1, TILE):
        for l0 in range(0, feat1, LANES):
            attend(q1, k1, v1, a1, bias, 0, c0, l0, rows1, me * rows1, n * rows1, cols1)
    loads[4].wait()
    loads[5].wait()
    y1 = gated(
        x1[...].reshape(rows1 * cols1, feat1), mod1, a1[...].reshape(rows1 * cols1, feat1), out1
    )
    x2 = merge(y1, merge1, rows1, cols1)

    loads[6].wait()
    h2 = modulate(x2.astype(F32), mod2)
    inner = HEADS2 * DH
    slot = lax.rem(me, HEADS2)
    base = me - slot
    pair = count2 // 2
    kv = dot(h2, qkv2[:, inner:])
    for h in range(HEADS2):
        k = kv[:, h * DH : (h + 1) * DH]
        v = kv[:, inner + h * DH : inner + (h + 1) * DH]
        kv_out[h] = jnp.concatenate([k, v], axis=1).astype(BF16)

    def kv_copy(p):
        peer = lax.rem(me + p, n)
        return remote(
            kv_out.at[lax.rem(peer, HEADS2)], kv_all.at[me], kv_send.at[p], kv_recv.at[me], peer
        )

    def kv_from(p):
        peer = lax.rem(me + p, n)
        return remote(kv_out.at[0], kv_all.at[peer], kv_send.at[p], kv_recv.at[peer], peer)

    def q_copy(p):
        other = lax.rem(slot + p, HEADS2)
        return remote(
            q_out.at[other], q_all.at[slot], q_send.at[p], q_recv.at[slot], base + other
        )

    def q_from(p):
        other = lax.rem(slot + p, HEADS2)
        return remote(q_out.at[0], q_all.at[other], q_send.at[p], q_recv.at[other], base + other)

    def o_copy(other):
        return remote(
            o_out.at[other], o_all.at[slot], o_send.at[other], o_recv.at[slot], base + other
        )

    def o_from(p):
        other = lax.rem(slot + p, HEADS2)
        return remote(o_out.at[0], o_all.at[other], o_send.at[other], o_recv.at[other], base + other)

    def each(count, make, act):
        def step(p, carry):
            act(make(p))
            return carry

        lax.fori_loop(1, count, step, 0)


    def far_first(i, carry):
        p = lax.rem(i + n // 2 - HEADS2 // 2, n)

        @pl.when(p > 0)
        def _():
            kv_copy(p).start()

        return carry

    lax.fori_loop(0, n, far_first, 0)
    q = dot(h2, qkv2[:, :inner]).astype(BF16).astype(F32) * scale
    for h in range(HEADS2):
        mine = q[:, h * DH : (h + 1) * DH]
        q_out[h] = jnp.concatenate([mine[:pair], mine[pair:]], axis=1).astype(BF16)
    each(HEADS2, q_copy, lambda c: c.start())
    kv_all[me] = kv_out[slot]
    q_all[slot] = q_out[slot]
    each(HEADS2, q_from, lambda c: c.wait_recv())
    each(n, kv_from, lambda c: c.wait_recv())

    piece = min(n, 16)
    packed = q_all[...].astype(F32)
    blank = jnp.zeros((HEADS2, pair, DH), F32)
    queries = jnp.concatenate(
        [
            jnp.concatenate([packed[:, :, :DH], blank], axis=2),
            jnp.concatenate([packed[:, :, DH:], blank], axis=2),
        ],
        axis=1,
    )
    queries = queries.astype(BF16).reshape(HEADS2 * count2, 2 * DH)
    block = 128

    for b in range(HEADS2 * count2 // block):
        asked = queries[b * block : (b + 1) * block]

        def keys_step(t, carry):
            top, total, summed = carry
            kv = kv_all[pl.ds(t * piece, piece)].reshape(piece * count2, 2 * DH)
            s = dot_t(asked, kv)
            new = jnp.maximum(top, jnp.max(s, axis=-1, keepdims=True))
            fade = jnp.exp(top - new)
            e = jnp.exp(s - new)
            return (
                new,
                total * fade + jnp.sum(e, axis=-1, keepdims=True),
                summed * fade + dot(e.astype(BF16), kv),
            )

        start = (
            jnp.full((block, 1), NEGATIVE, F32),
            jnp.zeros((block, 1), F32),
            jnp.zeros((block, 2 * DH), F32),
        )
        if n == piece:
            _, total, summed = keys_step(0, start)
        else:
            _, total, summed = lax.fori_loop(0, n // piece, keys_step, start)
        per = block // count2
        o = (summed * (1.0 / total)).reshape(per, count2, 2 * DH)
        o_out[b * per : (b + 1) * per] = jnp.concatenate(
            [o[:, :pair, DH:], o[:, pair:, DH:]], axis=2
        ).astype(BF16)
        for other in range(b * per, (b + 1) * per):

            @pl.when(other != slot)
            def _():
                o_copy(other).start()

    o_all[slot] = o_out[slot]
    loads[7].wait()
    each(HEADS2, o_from, lambda c: c.wait_recv())
    packed = o_all[...].astype(F32)
    attended = jnp.concatenate(
        [
            jnp.concatenate([packed[h, :, :DH], packed[h, :, DH:]], axis=0)
            for h in range(HEADS2)
        ],
        axis=1,
    )
    result[...] = gated(x2, mod2, attended.astype(BF16), out2).reshape(rows2, cols2, x2.shape[1])

    @pl.when(has_below)
    def _():
        for copy in (down0[0], down1[0], down1[1]):
            copy.wait_send()

    @pl.when(has_above)
    def _():
        for copy in (up0[0], up1[0], up1[1]):
            copy.wait_send()

    each(n, kv_copy, lambda c: c.wait_send())
    each(HEADS2, q_copy, lambda c: c.wait_send())
    each(HEADS2, o_from, lambda c: c.wait_send())


def on_device(n, *args):
    tok, _, w_qkv0, w_out0, w_merge0, _, w_qkv1, w_out1, w_merge1, _, w_qkv2, w_out2 = args
    rows0, cols0, feat0 = tok.shape
    rows1, cols1, feat1 = rows0 // 2, cols0 // 2, w_merge0.shape[1]
    rows2, cols2, feat2 = rows1 // 2, cols1 // 2, w_merge1.shape[1]
    count2 = rows2 * cols2
    weights = [w_qkv0, w_out0, w_merge0, w_qkv1, w_out1, w_merge1, w_qkv2, w_out2]

    def vm(*shape):
        return pltpu.VMEM(shape, BF16)

    any_spec = pl.BlockSpec(memory_space=pl.ANY)
    vmem = pl.BlockSpec(memory_space=pltpu.VMEM)
    return pl.pallas_call(
        functools.partial(kernel, n),
        out_shape=jax.ShapeDtypeStruct((rows2, cols2, feat2), BF16),
        in_specs=[vmem if i in (1, 5, 9) else any_spec for i in range(12)],
        out_specs=vmem,
        scratch_shapes=[vm(*w.shape) for w in weights]
        + [pltpu.SemaphoreType.DMA((9,))]
        + [
            vm(rows0, cols0, feat0),
            vm(2 * HALO, cols0, feat0),
            vm(rows0, cols0, feat0),
            vm(rows0 + 2 * HALO, cols0 + 2 * PAD, feat0),
            vm(rows0 + 2 * HALO, cols0 + 2 * PAD, feat0),
            vm(rows0, cols0, feat0),
            vm(rows1, cols1, feat1),
            vm(2 * HALO, cols1, feat1),
            vm(rows1, cols1, feat1),
            vm(rows1 + 2 * HALO, cols1 + 2 * PAD, feat1),
            vm(rows1 + 2 * HALO, cols1 + 2 * PAD, feat1),
            vm(rows1, cols1, feat1),
            vm(HEADS2, count2, 2 * DH),
            vm(HEADS2, count2 // 2, 2 * DH),
            vm(HEADS2, count2 // 2, 2 * DH),
            vm(n, count2, 2 * DH),
            vm(HEADS2, count2 // 2, 2 * DH),
            vm(HEADS2, count2 // 2, 2 * DH),
        ]
        + [pltpu.SemaphoreType.DMA((4,))] * 4
        + [pltpu.SemaphoreType.DMA((n,))] * 2
        + [pltpu.SemaphoreType.DMA((HEADS2,))] * 4,
        compiler_params=pltpu.CompilerParams(
            collective_id=0, has_side_effects=True, vmem_limit_bytes=56 * 1024 * 1024
        ),
    )(*args)


def solution(mesh):
    return jax.shard_map(
        functools.partial(on_device, mesh.shape["row"]),
        mesh=mesh,
        in_specs=(
            P(("groups", "row"), None, None),
            P("groups", None),
            P(),
            P(),
            P(),
            P("groups", None),
            P(),
            P(),
            P(),
            P("groups", None),
            P(),
            P(),
        ),
        out_specs=P(("groups", "row"), None, None),
        check_vma=False,
    )
```
